512 devices in a mesh: row: 32 (over z, x), col: 8 (over y), mat: 2 (over core).
Axes of the slice: x: 4, y: 8, z: 8, core: 2. Of those that a mesh axis runs over, the one named last changes fastest.
Arguments:
- weight: bfloat16 [2, 8192, 14336], P('mat', 'row', 'col'), may hold values from -6 to 6
- gradient: bfloat16 [2, 8192, 14336], P('mat', 'row', 'col'), may hold values from -600 to 600
- momentum: bfloat16 [2, 8192, 14336], P('mat', 'row', 'col'), may hold values from -6 to 6
- basis_in: float32 [2, 14336, 512], P('mat', ('col', 'row')), may hold values from -6 to 6
Outputs:
- new_weight: bfloat16 [2, 8192, 14336], P('mat', 'row', 'col')
- new_momentum: bfloat16 [2, 8192, 14336], P('mat', 'row', 'col')
- new_basis: float32 [2, 14336, 512], P('mat', ('col', 'row'))
The draws below stay inside these ranges and needn't reach their ends.
All inputs are finite; a program needn't handle non-finite values.
Results may differ from the reference program's by a relative error of at most 0.006.
Values may be sent and summed in bfloat16 or wider, within the bound.
No kernel may reach another device: no remote copies, remote signals or barrier semaphores. Data moves between devices by JAX's collectives and lax.ppermute only.
A program may use at most 64 MiB of HBM per device.

```python
import math
import jax
import jax.numpy as jnp
from jax import lax

ROWS = 8192
COLS = 14336
RANK = 512


def draw_gradient(key, part):
    key = jax.random.fold_in(key, 11)
    first, second, third = jax.random.split(key, 3)
    row_pos = jnp.arange(ROWS, dtype=jnp.float32) / (ROWS - 1)
    col_pos = jnp.arange(COLS, dtype=jnp.float32) / (COLS - 1)
    base = jnp.clip(jax.random.normal(first, (2, ROWS, COLS), jnp.float32), -6.0, 6.0)
    row_scale = 10.0 ** (0.5 * row_pos + 0.5 * jax.random.uniform(second, (ROWS,), jnp.float32))
    col_scale = 3.0 ** col_pos * 2.0 ** jax.random.uniform(third, (COLS,), jnp.float32)
    mat_scale = jnp.array([1.0, 1.6], jnp.float32)
    return (base * row_scale[None, :, None] * col_scale[None, None, :] * mat_scale[:, None, None]).astype(jnp.bfloat16)


def shard_levels(stream_key, extent, pieces, smallest, top_value):
    def one(axis_at, parts):
        steps = jax.random.uniform(jax.random.fold_in(jax.random.fold_in(stream_key, 6), axis_at), (parts,), jnp.float32, smallest / len(pieces), top_value / len(pieces))
        return jnp.repeat(jnp.exp(steps), extent[axis_at] // parts).reshape((-1,) + (1,) * (len(extent) - axis_at - 1))

    level = one(*pieces[0])
    for cut in pieces[1:]:
        level = level * one(*cut)
    return level


def gaussian(own_key, dims, scale, reach, cuts=(), kind=jnp.bfloat16):
    entries = jax.random.normal(own_key, dims, jnp.float32) * scale
    if len(cuts) > 0:
        entries = shard_levels(own_key, dims, cuts, -0.22, 0.18) * entries
    return jnp.clip(entries, min=-reach, max=reach).astype(kind)


def setup_inputs(seed: int = 0) -> dict:
    key_list = jax.random.split(jax.random.key(seed), 5)
    return {
        "weight": gaussian(key_list[0], (2, ROWS, COLS), 1.0, 6.0, ((0, 2), (1, 32), (2, 8))),
        "gradient": draw_gradient(jax.random.fold_in(key_list[4], 71), 0),
        "momentum": gaussian(key_list[2], (2, ROWS, COLS), 1.0, 6.0, ((0, 2), (1, 32), (2, 8))),
        "basis_in": gaussian(key_list[3], (2, COLS, RANK), 1.0, 6.0, ((0, 2), (1, 256)), jnp.float32),
    }


momentum_keep = 0.95
step_size = 0.25
epsilon = 1e-06

def one_matrix(weight_local, blend32, basis_prev):
    blended = blend32.astype(jnp.bfloat16)
    left = jnp.dot(blended.astype(jnp.float32), basis_prev.astype(jnp.bfloat16).astype(jnp.float32), preferred_element_type=jnp.float32)
    gram_matrix = lax.dot_general(left, left, (((0,), (0,)), ((), ())), precision=lax.Precision.HIGHEST)
    chol_factor = jnp.linalg.cholesky(gram_matrix)
    ortho = jax.scipy.linalg.solve_triangular(chol_factor, left.T, lower=True).T
    ortho_low = ortho.astype(jnp.bfloat16)
    right_factor = lax.dot_general(blended.astype(jnp.float32), ortho_low.astype(jnp.float32), (((0,), (0,)), ((), ())), preferred_element_type=jnp.float32)
    column_squares = lax.optimization_barrier(jnp.sum(right_factor * right_factor, axis=0))
    new_basis = right_factor * (math.sqrt(COLS) * lax.rsqrt(column_squares + epsilon))
    feedback = lax.dot_general(ortho, right_factor, (((1,), (1,)), ((), ())), precision=lax.Precision.HIGHEST)
    new_momentum = (blend32 - (1.0 - momentum_keep) * feedback).astype(jnp.bfloat16)
    update = lax.dot_general(ortho, new_basis, (((1,), (1,)), ((), ())), precision=lax.Precision.HIGHEST)
    factor = step_size * math.sqrt(ROWS / RANK)
    new_weight = (weight_local.astype(jnp.float32) - factor * update).astype(jnp.bfloat16)
    return (new_weight, new_momentum, new_basis)

def reference(weight, gradient, momentum, basis_in):
    grads = gradient.astype(jnp.float32)
    square_total = jnp.sum(grads * grads)
    root_mean = jnp.sqrt(square_total / (2.0 * ROWS * COLS))
    clip_scale = 1.0 / jnp.maximum(1.0, root_mean)
    weights_out = []
    moments_out = []
    bases_out = []
    for which in range(2):
        blend32 = momentum[which].astype(jnp.float32) + clip_scale * grads[which]
        new_weight, new_momentum, new_basis = one_matrix(weight[which], blend32, basis_in[which])
        weights_out.append(new_weight)
        moments_out.append(new_momentum)
        bases_out.append(new_basis)
    return (jnp.stack(weights_out), jnp.stack(moments_out), jnp.stack(bases_out))
```

```python
import functools
import math

import jax
import jax.numpy as jnp
from jax import lax
from jax.experimental import pallas as pl
from jax.experimental.pallas import tpu as pltpu
from jax.sharding import Mesh
from jax.sharding import PartitionSpec as P

ROWS = 8192
COLS = 14336
RANK = 512
BLOCK = 128
PIVOTS = 8

momentum_keep = 0.95
step_size = 0.25
epsilon = 1e-06

f32 = jnp.float32
bf16 = jnp.bfloat16
HIGHEST = lax.Precision.HIGHEST
TN = (((0,), (0,)), ((), ()))
NT = (((1,), (1,)), ((), ()))


def block_inverse(block):
    tiles = BLOCK // 8
    full = (8, BLOCK)
    work = [block[8 * v : 8 * v + 8, :] for v in range(tiles)]
    row = lax.broadcasted_iota(jnp.int32, full, 0)
    lane = lax.broadcasted_iota(jnp.int32, full, 1)
    inverse = [jnp.where(lane == row + 8 * v, 1.0, 0.0).astype(f32) for v in range(tiles)]
    scale = [None] * tiles

    def across(tile, j):
        return jnp.broadcast_to(tile[:, j : j + 1], full)

    def down(tile, s):
        return jnp.broadcast_to(tile[s : s + 1, :], full)

    for j in range(0, BLOCK, PIVOTS):
        at, s = divmod(j, 8)
        first = [across(work[at], j + a) for a in range(PIVOTS)]
        pivot = [[down(first[b], s + a) for b in range(a + 1)] for a in range(PIVOTS)]
        rows = [down(work[at], s + a) for a in range(PIVOTS)]
        rows_inv = [down(inverse[at], s + a) for a in range(PIVOTS)]
        lower = [[None] * PIVOTS for _ in range(PIVOTS)]
        recip = [None] * PIVOTS
        for a in range(PIVOTS):
            recip[a] = 1.0 / pivot[a][a]
            root = lax.rsqrt(pivot[a][a])
            scale[at] = root if s + a == 0 else jnp.where(row >= s + a, root, scale[at])
            for i in range(a + 1, PIVOTS):
                lower[i][a] = pivot[i][a] * recip[a]
                for b in range(a + 1, i + 1):
                    pivot[i][b] = pivot[i][b] - lower[i][a] * pivot[b][a]
                rows[i] = rows[i] - lower[i][a] * rows[a]
                rows_inv[i] = rows_inv[i] - lower[i][a] * rows_inv[a]
        unit = [rows[a] * recip[a] for a in range(PIVOTS)]
        unit_inv = [rows_inv[a] * recip[a] for a in range(PIVOTS)]
        for v in range(at, tiles):
            column = first if v == at else [across(work[v], j + a) for a in range(PIVOTS)]
            column = list(column)
            for a in range(PIVOTS):
                for i in range(a + 1, PIVOTS):
                    column[i] = column[i] - lower[i][a] * column[a]
            for a in range(PIVOTS):
                factor = column[a]
                if v == at:
                    if s + a == 7:
                        continue
                    factor = jnp.where(row > s + a, factor, 0.0)
                if not (v == at and s + PIVOTS == 8):
                    work[v] = work[v] - factor * unit[a]
                inverse[v] = inverse[v] - factor * unit_inv[a]
    return jnp.concatenate([inverse[v] * scale[v] for v in range(tiles)], axis=0)


def chol_inverse_kernel(gram_ref, out_ref, work_ref):
    work_ref[:, :RANK] = gram_ref[...]
    i = lax.broadcasted_iota(jnp.int32, (RANK, RANK), 0)
    j = lax.broadcasted_iota(jnp.int32, (RANK, RANK), 1)
    work_ref[:, RANK:] = jnp.where(i == j, 1.0, 0.0).astype(f32)
    for k in range(0, RANK, BLOCK):
        end = k + BLOCK
        left = RANK - end
        inverse = block_inverse(work_ref[k:end, k:end])
        wide = jnp.dot(
            inverse, work_ref[k:end, end : RANK + end], precision=HIGHEST, preferred_element_type=f32
        )
        out_ref[k:end, :end] = wide[:, left:]
        if left:
            out_ref[k:end, end:] = jnp.zeros((BLOCK, left), f32)
            work_ref[end:, end : RANK + end] = work_ref[end:, end : RANK + end] - lax.dot_general(
                wide[:, :left], wide, TN, precision=HIGHEST, preferred_element_type=f32
            )


def chol_inverse(gram):
    return pl.pallas_call(
        chol_inverse_kernel,
        out_shape=jax.ShapeDtypeStruct((RANK, RANK), f32),
        in_specs=[pl.BlockSpec(memory_space=pltpu.VMEM)],
        out_specs=pl.BlockSpec(memory_space=pltpu.VMEM),
        scratch_shapes=[pltpu.VMEM((RANK, 2 * RANK), f32)],
        compiler_params=pltpu.CompilerParams(vmem_limit_bytes=16 * 2**20),
        cost_estimate=pl.CostEstimate(flops=2 * 10**9, bytes_accessed=2 * 2**20, transcendentals=0),
        name="chol_inverse",
    )(gram)


def swap_sum(x, axis, dim):
    return jnp.sum(lax.all_to_all(x, axis, dim, dim, tiled=True), axis=dim)


def spread_sum(x, axis, size):
    return swap_sum(jnp.broadcast_to(x[None], (size,) + x.shape), axis, 0)


def on_device(weight, gradient, momentum, basis_in):
    weight_local = weight[0]
    grads = gradient[0].astype(f32)
    basis_low = basis_in[0].astype(bf16)
    basis_x = lax.all_gather(basis_low, "x", axis=0, tiled=True)
    basis_all = lax.all_gather(basis_x, "z", axis=0, tiled=True)

    squares = jnp.full((1, 128), jnp.sum(grads * grads), f32)
    squares = spread_sum(squares, ("z", "x"), 32)
    squares = spread_sum(squares, "y", 8)
    square_total = lax.psum(squares[0, 0], "core")
    root_mean = jnp.sqrt(square_total / (2.0 * ROWS * COLS))
    clip_scale = 1.0 / jnp.maximum(1.0, root_mean)
    blend32 = momentum[0].astype(f32) + clip_scale * grads
    blended = blend32.astype(bf16)

    partial_left = jnp.dot(blended, basis_all, preferred_element_type=f32)
    left_rows = swap_sum(partial_left.reshape(8, 32, RANK), "y", 0)
    left = lax.all_gather(left_rows, "y", axis=0, tiled=True)

    gram_part = lax.dot_general(left, left, TN, precision=HIGHEST)
    gram_part = lax.dynamic_slice_in_dim(gram_part, lax.axis_index("y") * 64, 64, axis=0)
    gram_rows = swap_sum(gram_part.reshape(4, 16, RANK), "x", 0)
    gram_rows = spread_sum(gram_rows, "z", 8)
    gram_rows = lax.all_gather(gram_rows, "x", axis=0, tiled=True)
    gram_matrix = lax.all_gather(gram_rows, "y", axis=0, tiled=True)

    high = lax.reduce_precision(left, 8, 7)
    low = (left - high).astype(bf16)
    high = high.astype(bf16)
    product = lax.dot_general(blended, high, TN, preferred_element_type=f32)
    product = product + lax.dot_general(blended, low, TN, preferred_element_type=f32)
    product = swap_sum(product.reshape(8, 4, 56, RANK), "x", 1)
    product = swap_sum(product, "z", 0)
    product_all = lax.all_gather(product.astype(bf16), "x", axis=0, tiled=True)
    product_all = lax.all_gather(product_all, "z", axis=0, tiled=True)

    inverse_factor = chol_inverse(gram_matrix)
    ortho = lax.dot_general(left, inverse_factor, NT, precision=HIGHEST)
    right_own = lax.dot_general(product, inverse_factor, NT, precision=HIGHEST)
    right_all = lax.dot_general(product_all.astype(f32), inverse_factor, NT, precision=HIGHEST)

    column_squares = spread_sum(jnp.sum(right_all * right_all, axis=0, keepdims=True), "y", 8)
    right_low = right_all.astype(bf16)
    feedback = lax.dot_general(ortho.astype(bf16), right_low, NT, preferred_element_type=f32)
    new_momentum = (blend32 - (1.0 - momentum_keep) * feedback).astype(bf16)
    stretch = math.sqrt(COLS) * lax.rsqrt(column_squares + epsilon)
    new_basis = right_own * stretch
    factor = step_size * math.sqrt(ROWS / RANK)
    update = lax.dot_general(
        (ortho * stretch).astype(bf16), right_low, NT, preferred_element_type=f32
    )
    new_weight = (weight_local.astype(f32) - factor * update).astype(bf16)
    return (new_weight[None], new_momentum[None], new_basis[None])


def solution(mesh):
    devices = mesh.devices.reshape(8, 4, 8, 2)
    fine = Mesh(devices, ("z", "x", "y", "core"))
    matrix = P("core", ("z", "x"), "y")
    basis = P("core", ("y", "z", "x"), None)
    return jax.shard_map(
        on_device,
        mesh=fine,
        in_specs=(matrix, matrix, matrix, basis),
        out_specs=(matrix, matrix, basis),
        check_vma=False,
    )
```

```python
import functools
import math

import jax
import jax.numpy as jnp
from jax import lax
from jax.experimental import pallas as pl
from jax.experimental.pallas import tpu as pltpu
from jax.sharding import Mesh
from jax.sharding import PartitionSpec as P

ROWS = 8192
COLS = 14336
RANK = 512
BLOCK = 128
PIVOTS = 8

momentum_keep = 0.95
step_size = 0.25
epsilon = 1e-06

f32 = jnp.float32
bf16 = jnp.bfloat16
HIGHEST = lax.Precision.HIGHEST
TN = (((0,), (0,)), ((), ()))
NT = (((1,), (1,)), ((), ()))


def block_inverse(block):
    tiles = BLOCK // 8
    full = (8, BLOCK)
    work = [block[8 * v : 8 * v + 8, :] for v in range(tiles)]
    row = lax.broadcasted_iota(jnp.int32, full, 0)
    lane = lax.broadcasted_iota(jnp.int32, full, 1)
    inverse = [jnp.where(lane == row + 8 * v, 1.0, 0.0).astype(f32) for v in range(tiles)]
    scale = [None] * tiles

    def across(tile, j):
        return jnp.broadcast_to(tile[:, j : j + 1], full)

    def down(tile, s):
        return jnp.broadcast_to(tile[s : s + 1, :], full)

    for j in range(0, BLOCK, PIVOTS):
        at, s = divmod(j, 8)
        first = [across(work[at], j + a) for a in range(PIVOTS)]
        pivot = [[down(first[b], s + a) for b in range(a + 1)] for a in range(PIVOTS)]
        rows = [down(work[at], s + a) for a in range(PIVOTS)]
        rows_inv = [down(inverse[at], s + a) for a in range(PIVOTS)]
        lower = [[None] * PIVOTS for _ in range(PIVOTS)]
        recip = [None] * PIVOTS
        for a in range(PIVOTS):
            recip[a] = 1.0 / pivot[a][a]
            root = lax.rsqrt(pivot[a][a])
            scale[at] = root if s + a == 0 else jnp.where(row >= s + a, root, scale[at])
            for i in range(a + 1, PIVOTS):
                lower[i][a] = pivot[i][a] * recip[a]
                for b in range(a + 1, i + 1):
                    pivot[i][b] = pivot[i][b] - lower[i][a] * pivot[b][a]
                rows[i] = rows[i] - lower[i][a] * rows[a]
                rows_inv[i] = rows_inv[i] - lower[i][a] * rows_inv[a]
        unit = [rows[a] * recip[a] for a in range(PIVOTS)]
        unit_inv = [rows_inv[a] * recip[a] for a in range(PIVOTS)]
        for v in range(at, tiles):
            column = first if v == at else [across(work[v], j + a) for a in range(PIVOTS)]
            column = list(column)
            for a in range(PIVOTS):
                for i in range(a + 1, PIVOTS):
                    column[i] = column[i] - lower[i][a] * column[a]
            for a in range(PIVOTS):
                factor = column[a]
                if v == at:
                    if s + a == 7:
                        continue
                    factor = jnp.where(row > s + a, factor, 0.0)
                if not (v == at and s + PIVOTS == 8):
                    work[v] = work[v] - factor * unit[a]
                inverse[v] = inverse[v] - factor * unit_inv[a]
    return jnp.concatenate([inverse[v] * scale[v] for v in range(tiles)], axis=0)


def chol_inverse_kernel(gram_ref, out_ref, work_ref):
    work_ref[:, :RANK] = gram_ref[...]
    i = lax.broadcasted_iota(jnp.int32, (RANK, RANK), 0)
    j = lax.broadcasted_iota(jnp.int32, (RANK, RANK), 1)
    work_ref[:, RANK:] = jnp.where(i == j, 1.0, 0.0).astype(f32)
    for k in range(0, RANK, BLOCK):
        end = k + BLOCK
        left = RANK - end
        inverse = block_inverse(work_ref[k:end, k:end])
        wide = jnp.dot(
            inverse, work_ref[k:end, end : RANK + end], precision=HIGHEST, preferred_element_type=f32
        )
        out_ref[k:end, :end] = wide[:, left:]
        if left:
            out_ref[k:end, end:] = jnp.zeros((BLOCK, left), f32)
            work_ref[end:, end : RANK + end] = work_ref[end:, end : RANK + end] - lax.dot_general(
                wide[:, :left], wide, TN, precision=HIGHEST, preferred_element_type=f32
            )


def chol_inverse(gram):
    return pl.pallas_call(
        chol_inverse_kernel,
        out_shape=jax.ShapeDtypeStruct((RANK, RANK), f32),
        in_specs=[pl.BlockSpec(memory_space=pltpu.VMEM)],
        out_specs=pl.BlockSpec(memory_space=pltpu.VMEM),
        scratch_shapes=[pltpu.VMEM((RANK, 2 * RANK), f32)],
        compiler_params=pltpu.CompilerParams(vmem_limit_bytes=16 * 2**20),
        cost_estimate=pl.CostEstimate(flops=2 * 10**9, bytes_accessed=2 * 2**20, transcendentals=0),
        name="chol_inverse",
    )(gram)


def swap(x, axis):
    return lax.all_to_all(x, axis, 0, 0, tiled=True)


def spread(x, axis):
    size = lax.axis_size(axis)
    return swap(jnp.broadcast_to(x[None], (size,) + x.shape), axis)


def three_parts(x):
    high = lax.reduce_precision(x, 8, 7)
    rest = x - high
    middle = lax.reduce_precision(rest, 8, 7)
    return high.astype(bf16), middle.astype(bf16), (rest - middle).astype(bf16)


def natural(x):
    return x.reshape(4, 8, 56, RANK).transpose(1, 0, 2, 3).reshape(8 * 4 * 56, RANK)


def on_device(weight, gradient, momentum, basis_in):
    weight_local = weight[0]
    grads = gradient[0].astype(f32)
    basis_low = basis_in[0].astype(bf16)

    basis_z = spread(basis_low, "z").reshape(448, RANK)
    basis_all = natural(lax.all_gather(basis_z, "x", axis=0, tiled=True))
    squares = jnp.full((1, 128), jnp.sum(grads * grads), f32)
    squares, _ = lax.optimization_barrier((squares, basis_z))
    squares = jnp.sum(spread(squares, ("z", "x")), axis=0)
    squares = jnp.sum(spread(squares, "y"), axis=0)
    square_total = lax.psum(squares, "core")[0, 0]

    root_mean = jnp.sqrt(square_total / (2.0 * ROWS * COLS))
    clip_scale = 1.0 / jnp.maximum(1.0, root_mean)
    blend32 = momentum[0].astype(f32) + clip_scale * grads
    blended = blend32.astype(bf16)

    partial_left = jnp.dot(blended, basis_all, preferred_element_type=f32)
    left_rows = jnp.sum(swap(partial_left.reshape(8, 32, RANK), "y"), axis=0)
    left = spread(left_rows, "y").reshape(256, RANK)

    gram_part = lax.dot_general(left, left, TN, precision=HIGHEST)
    gram_part = lax.dynamic_slice_in_dim(
        gram_part.reshape(4, 8, 16, RANK), lax.axis_index("y"), 1, axis=1
    ).reshape(4, 16, RANK)
    high, low = three_parts(left)[:2]
    product = lax.dot_general(blended, high, TN, preferred_element_type=f32)
    product = product + lax.dot_general(blended, low, TN, preferred_element_type=f32)
    product = product.astype(bf16).reshape(8, 4, 56, RANK).transpose(1, 0, 2, 3)

    gram_rows = jnp.sum(swap(gram_part, "x"), axis=0)
    product = jnp.sum(swap(product.reshape(4, 448, RANK), "x").astype(f32), axis=0)
    product = jnp.sum(swap(product.reshape(8, 56, RANK), "z"), axis=0)
    product_low = product.astype(bf16)
    product_all = lax.all_gather(product_low, ("z", "x"), axis=0, tiled=True)
    gram_rows, _ = lax.optimization_barrier((gram_rows, product_low))
    gram_rows = jnp.sum(spread(gram_rows, "z"), axis=0)
    gram_rows = spread(gram_rows, "y").reshape(128, RANK)
    gram_matrix = spread(gram_rows, "x").reshape(RANK, RANK)
    inverse_factor = chol_inverse(gram_matrix)

    ortho = lax.dot_general(left, inverse_factor, NT, precision=HIGHEST)
    right_own = lax.dot_general(product, inverse_factor, NT, precision=HIGHEST)
    high, low = three_parts(inverse_factor)[:2]
    right_all = lax.dot_general(product_all, high, NT, preferred_element_type=f32)
    right_all = right_all + lax.dot_general(product_all, low, NT, preferred_element_type=f32)

    column_squares = jnp.sum(right_all * right_all, axis=0, keepdims=True)
    column_squares = jnp.sum(spread(column_squares, "y"), axis=0)
    right_low = right_all.astype(bf16)
    feedback = lax.dot_general(ortho.astype(bf16), right_low, NT, preferred_element_type=f32)
    new_momentum = (blend32 - (1.0 - momentum_keep) * feedback).astype(bf16)
    stretch = math.sqrt(COLS) * lax.rsqrt(column_squares + epsilon)
    new_basis = right_own * stretch
    factor = step_size * math.sqrt(ROWS / RANK)
    update = lax.dot_general(
        (ortho * stretch).astype(bf16), right_low, NT, preferred_element_type=f32
    )
    new_weight = (weight_local.astype(f32) - factor * update).astype(bf16)
    return (new_weight[None], new_momentum[None], new_basis[None])


def solution(mesh):
    devices = mesh.devices.reshape(8, 4, 8, 2)
    fine = Mesh(devices, ("z", "x", "y", "core"))
    matrix = P("core", ("z", "x"), "y")
    basis = P("core", ("y", "z", "x"), None)
    return jax.shard_map(
        on_device,
        mesh=fine,
        in_specs=(matrix, matrix, matrix, basis),
        out_specs=(matrix, matrix, basis),
        check_vma=False,
    )
```

```python
import functools
import math

import jax
import jax.numpy as jnp
from jax import lax
from jax.experimental import pallas as pl
from jax.experimental.pallas import tpu as pltpu
from jax.sharding import Mesh
from jax.sharding import PartitionSpec as P

ROWS = 8192
COLS = 14336
RANK = 512
BLOCK = 128
PIVOTS = 8

momentum_keep = 0.95
step_size = 0.25
epsilon = 1e-06

f32 = jnp.float32
bf16 = jnp.bfloat16
HIGHEST = lax.Precision.HIGHEST
TN = (((0,), (0,)), ((), ()))
NT = (((1,), (1,)), ((), ()))


def block_inverse(block):
    tiles = BLOCK // 8
    full = (8, BLOCK)
    work = [block[8 * v : 8 * v + 8, :] for v in range(tiles)]
    row = lax.broadcasted_iota(jnp.int32, full, 0)
    lane = lax.broadcasted_iota(jnp.int32, full, 1)
    inverse = [jnp.where(lane == row + 8 * v, 1.0, 0.0).astype(f32) for v in range(tiles)]
    scale = [None] * tiles

    def across(tile, j):
        return jnp.broadcast_to(tile[:, j : j + 1], full)

    def down(tile, s):
        return jnp.broadcast_to(tile[s : s + 1, :], full)

    for j in range(0, BLOCK, PIVOTS):
        at, s = divmod(j, 8)
        first = [across(work[at], j + a) for a in range(PIVOTS)]
        pivot = [[down(first[b], s + a) for b in range(a + 1)] for a in range(PIVOTS)]
        rows = [down(work[at], s + a) for a in range(PIVOTS)]
        rows_inv = [down(inverse[at], s + a) for a in range(PIVOTS)]
        lower = [[None] * PIVOTS for _ in range(PIVOTS)]
        recip = [None] * PIVOTS
        for a in range(PIVOTS):
            recip[a] = 1.0 / pivot[a][a]
            root = lax.rsqrt(pivot[a][a])
            scale[at] = root if s + a == 0 else jnp.where(row >= s + a, root, scale[at])
            for i in range(a + 1, PIVOTS):
                lower[i][a] = pivot[i][a] * recip[a]
                for b in range(a + 1, i + 1):
                    pivot[i][b] = pivot[i][b] - lower[i][a] * pivot[b][a]
                rows[i] = rows[i] - lower[i][a] * rows[a]
                rows_inv[i] = rows_inv[i] - lower[i][a] * rows_inv[a]
        unit = [rows[a] * recip[a] for a in range(PIVOTS)]
        unit_inv = [rows_inv[a] * recip[a] for a in range(PIVOTS)]
        for v in range(at, tiles):
            column = first if v == at else [across(work[v], j + a) for a in range(PIVOTS)]
            column = list(column)
            for a in range(PIVOTS):
                for i in range(a + 1, PIVOTS):
                    column[i] = column[i] - lower[i][a] * column[a]
            for a in range(PIVOTS):
                factor = column[a]
                if v == at:
                    if s + a == 7:
                        continue
                    factor = jnp.where(row > s + a, factor, 0.0)
                if not (v == at and s + PIVOTS == 8):
                    work[v] = work[v] - factor * unit[a]
                inverse[v] = inverse[v] - factor * unit_inv[a]
    return jnp.concatenate([inverse[v] * scale[v] for v in range(tiles)], axis=0)


def chol_inverse_kernel(gram_ref, out_ref, work_ref):
    work_ref[:, :RANK] = gram_ref[...]
    i = lax.broadcasted_iota(jnp.int32, (RANK, RANK), 0)
    j = lax.broadcasted_iota(jnp.int32, (RANK, RANK), 1)
    work_ref[:, RANK:] = jnp.where(i == j, 1.0, 0.0).astype(f32)
    for k in range(0, RANK, BLOCK):
        end = k + BLOCK
        left = RANK - end
        inverse = block_inverse(work_ref[k:end, k:end])
        wide = jnp.dot(
            inverse, work_ref[k:end, end : RANK + end], precision=HIGHEST, preferred_element_type=f32
        )
        out_ref[k:end, :end] = wide[:, left:]
        if left:
            out_ref[k:end, end:] = jnp.zeros((BLOCK, left), f32)
            work_ref[end:, end : RANK + end] = work_ref[end:, end : RANK + end] - lax.dot_general(
                wide[:, :left], wide, TN, precision=HIGHEST, preferred_element_type=f32
            )


def chol_inverse(gram):
    return pl.pallas_call(
        chol_inverse_kernel,
        out_shape=jax.ShapeDtypeStruct((RANK, RANK), f32),
        in_specs=[pl.BlockSpec(memory_space=pltpu.VMEM)],
        out_specs=pl.BlockSpec(memory_space=pltpu.VMEM),
        scratch_shapes=[pltpu.VMEM((RANK, 2 * RANK), f32)],
        compiler_params=pltpu.CompilerParams(vmem_limit_bytes=16 * 2**20),
        cost_estimate=pl.CostEstimate(flops=2 * 10**9, bytes_accessed=2 * 2**20, transcendentals=0),
        name="chol_inverse",
    )(gram)


def swap(x, axis):
    return lax.all_to_all(x, axis, 0, 0, tiled=True)


def spread(x, axis):
    size = lax.axis_size(axis)
    return swap(jnp.broadcast_to(x[None], (size,) + x.shape), axis)


def three_parts(x):
    high = lax.reduce_precision(x, 8, 7)
    rest = x - high
    middle = lax.reduce_precision(rest, 8, 7)
    return high.astype(bf16), middle.astype(bf16), (rest - middle).astype(bf16)


def from_parts(x):
    return x[:, :16].astype(f32) + (x[:, 16:32].astype(f32) + x[:, 32:].astype(f32))


def natural(x):
    return x.reshape(4, 8, 56, RANK).transpose(1, 0, 2, 3).reshape(8 * 4 * 56, RANK)


def on_device(weight, gradient, momentum, basis_in):
    weight_local = weight[0]
    grads = gradient[0].astype(f32)
    basis_low = basis_in[0].astype(bf16)

    basis_z = spread(basis_low, "z").reshape(448, RANK)
    basis_all = natural(lax.all_gather(basis_z, "x", axis=0, tiled=True))
    squares = jnp.full((1, 128), jnp.sum(grads * grads), f32)
    squares, _ = lax.optimization_barrier((squares, basis_z))
    squares = jnp.sum(spread(squares, ("z", "x")), axis=0)
    squares = jnp.sum(spread(squares, "y"), axis=0)
    square_total = lax.psum(squares, "core")[0, 0]

    root_mean = jnp.sqrt(square_total / (2.0 * ROWS * COLS))
    clip_scale = 1.0 / jnp.maximum(1.0, root_mean)
    blend32 = momentum[0].astype(f32) + clip_scale * grads
    blended = blend32.astype(bf16)

    partial_left = jnp.dot(blended, basis_all, preferred_element_type=f32)
    left_rows = jnp.sum(swap(partial_left.reshape(8, 32, RANK), "y"), axis=0)
    left = spread(left_rows, "y").reshape(256, RANK)

    gram_part = lax.dot_general(left, left, TN, precision=HIGHEST)
    gram_part = lax.dynamic_slice_in_dim(
        gram_part.reshape(4, 8, 16, RANK), lax.axis_index("y"), 1, axis=1
    ).reshape(4, 16, RANK)
    high, low = three_parts(left)[:2]
    product = lax.dot_general(blended, high, TN, preferred_element_type=f32)
    product = product + lax.dot_general(blended, low, TN, preferred_element_type=f32)
    product = product.astype(bf16).reshape(8, 4, 56, RANK).transpose(1, 0, 2, 3)

    both = jnp.concatenate((product.reshape(4, 448, RANK),) + three_parts(gram_part), axis=1)
    both = swap(both, "x")
    product = jnp.sum(both[:, :448].astype(f32), axis=0).astype(bf16).reshape(8, 56, RANK)
    gram_rows = jnp.concatenate(three_parts(jnp.sum(from_parts(both[:, 448:]), axis=0)), axis=0)
    both = jnp.concatenate((product, jnp.broadcast_to(gram_rows[None], (8, 48, RANK))), axis=1)
    both = swap(both, "z")
    product = jnp.sum(both[:, :56].astype(f32), axis=0)
    gram_rows = jnp.sum(from_parts(both[:, 56:]), axis=0)
    product_all = spread(product.astype(bf16), "x").reshape(224, RANK)
    gram_rows, product_all = lax.optimization_barrier((gram_rows, product_all))
    product_all = lax.all_gather(product_all, "z", axis=0, tiled=True)
    gram_rows = spread(gram_rows, "y").reshape(128, RANK)
    gram_matrix = spread(gram_rows, "x").reshape(RANK, RANK)
    inverse_factor = chol_inverse(gram_matrix)

    ortho = lax.dot_general(left, inverse_factor, NT, precision=HIGHEST)
    right_own = lax.dot_general(product, inverse_factor, NT, precision=HIGHEST)
    high, low = three_parts(inverse_factor)[:2]
    right_all = lax.dot_general(product_all, high, NT, preferred_element_type=f32)
    right_all = right_all + lax.dot_general(product_all, low, NT, preferred_element_type=f32)

    column_squares = jnp.sum(right_all * right_all, axis=0, keepdims=True)
    column_squares = jnp.sum(spread(column_squares, "y"), axis=0)
    right_low = right_all.astype(bf16)
    feedback = lax.dot_general(ortho.astype(bf16), right_low, NT, preferred_element_type=f32)
    new_momentum = (blend32 - (1.0 - momentum_keep) * feedback).astype(bf16)
    stretch = math.sqrt(COLS) * lax.rsqrt(column_squares + epsilon)
    new_basis = right_own * stretch
    factor = step_size * math.sqrt(ROWS / RANK)
    update = lax.dot_general(
        (ortho * stretch).astype(bf16), right_low, NT, preferred_element_type=f32
    )
    new_weight = (weight_local.astype(f32) - factor * update).astype(bf16)
    return (new_weight[None], new_momentum[None], new_basis[None])


def solution(mesh):
    devices = mesh.devices.reshape(8, 4, 8, 2)
    fine = Mesh(devices, ("z", "x", "y", "core"))
    matrix = P("core", ("z", "x"), "y")
    basis = P("core", ("y", "z", "x"), None)
    return jax.shard_map(
        on_device,
        mesh=fine,
        in_specs=(matrix, matrix, matrix, basis),
        out_specs=(matrix, matrix, basis),
        check_vma=False,
    )
```

```python
import functools
import math

import jax
import jax.numpy as jnp
from jax import lax
from jax.experimental import pallas as pl
from jax.experimental.pallas import tpu as pltpu
from jax.sharding import Mesh
from jax.sharding import PartitionSpec as P

ROWS = 8192
COLS = 14336
RANK = 512
BLOCK = 128
PIVOTS = 8

momentum_keep = 0.95
step_size = 0.25
epsilon = 1e-06

f32 = jnp.float32
bf16 = jnp.bfloat16
HIGHEST = lax.Precision.HIGHEST
NN = (((1,), (0,)), ((), ()))
TN = (((0,), (0,)), ((), ()))
NT = (((1,), (1,)), ((), ()))


def block_inverse(block):
    tiles = BLOCK // 8
    full = (8, BLOCK)
    work = [block[8 * v : 8 * v + 8, :] for v in range(tiles)]
    row = lax.broadcasted_iota(jnp.int32, full, 0)
    lane = lax.broadcasted_iota(jnp.int32, full, 1)
    inverse = [jnp.where(lane == row + 8 * v, 1.0, 0.0).astype(f32) for v in range(tiles)]
    scale = [None] * tiles

    def across(tile, j):
        return jnp.broadcast_to(tile[:, j : j + 1], full)

    def down(tile, s):
        return jnp.broadcast_to(tile[s : s + 1, :], full)

    for j in range(0, BLOCK, PIVOTS):
        at, s = divmod(j, 8)
        first = [across(work[at], j + a) for a in range(PIVOTS)]
        pivot = [[down(first[b], s + a) for b in range(a + 1)] for a in range(PIVOTS)]
        rows = [down(work[at], s + a) for a in range(PIVOTS)]
        rows_inv = [down(inverse[at], s + a) for a in range(PIVOTS)]
        lower = [[None] * PIVOTS for _ in range(PIVOTS)]
        recip = [None] * PIVOTS
        for a in range(PIVOTS):
            recip[a] = 1.0 / pivot[a][a]
            root = lax.rsqrt(pivot[a][a])
            scale[at] = root if s + a == 0 else jnp.where(row >= s + a, root, scale[at])
            for i in range(a + 1, PIVOTS):
                lower[i][a] = pivot[i][a] * recip[a]
                for b in range(a + 1, i + 1):
                    pivot[i][b] = pivot[i][b] - lower[i][a] * pivot[b][a]
                rows[i] = rows[i] - lower[i][a] * rows[a]
                rows_inv[i] = rows_inv[i] - lower[i][a] * rows_inv[a]
        unit = [rows[a] * recip[a] for a in range(PIVOTS)]
        unit_inv = [rows_inv[a] * recip[a] for a in range(PIVOTS)]
        for v in range(at, tiles):
            column = first if v == at else [across(work[v], j + a) for a in range(PIVOTS)]
            column = list(column)
            for a in range(PIVOTS):
                for i in range(a + 1, PIVOTS):
                    column[i] = column[i] - lower[i][a] * column[a]
            for a in range(PIVOTS):
                factor = column[a]
                if v == at:
                    if s + a == 7:
                        continue
                    factor = jnp.where(row > s + a, factor, 0.0)
                if not (v == at and s + PIVOTS == 8):
                    work[v] = work[v] - factor * unit[a]
                inverse[v] = inverse[v] - factor * unit_inv[a]
    return jnp.concatenate([inverse[v] * scale[v] for v in range(tiles)], axis=0)


def exact(a, b, dims):
    return lax.dot_general(a, b, dims, precision=HIGHEST, preferred_element_type=f32)


def chol_inverse_kernel(gram_ref, out_ref, work_ref):
    work_ref[:, :RANK] = gram_ref[...]
    i = lax.broadcasted_iota(jnp.int32, (RANK, RANK), 0)
    j = lax.broadcasted_iota(jnp.int32, (RANK, RANK), 1)
    work_ref[:, RANK:] = jnp.where(i == j, 1.0, 0.0).astype(f32)
    ahead = gram_ref[:BLOCK, :BLOCK]
    for k in range(0, RANK, BLOCK):
        end = k + BLOCK
        far = end + BLOCK
        left = RANK - far
        inverse = block_inverse(ahead)
        if end == RANK:
            out_ref[k:, :] = exact(inverse, work_ref[k:, end:], NN)
            break
        near = exact(inverse, work_ref[k:end, end:far], NN)
        ahead = work_ref[end:far, end:far] - exact(near, near, TN)
        wide = exact(inverse, work_ref[k:end, far : RANK + end], NN)
        work_ref[end:far, far : RANK + end] = work_ref[end:far, far : RANK + end] - exact(
            near, wide, TN
        )
        if left:
            work_ref[far:, far : RANK + end] = work_ref[far:, far : RANK + end] - exact(
                wide[:, :left], wide, TN
            )
        out_ref[k:end, :end] = wide[:, left:]
        out_ref[k:end, end:] = jnp.zeros((BLOCK, RANK - end), f32)


def chol_inverse(gram):
    return pl.pallas_call(
        chol_inverse_kernel,
        out_shape=jax.ShapeDtypeStruct((RANK, RANK), f32),
        in_specs=[pl.BlockSpec(memory_space=pltpu.VMEM)],
        out_specs=pl.BlockSpec(memory_space=pltpu.VMEM),
        scratch_shapes=[pltpu.VMEM((RANK, 2 * RANK), f32)],
        compiler_params=pltpu.CompilerParams(vmem_limit_bytes=16 * 2**20),
        cost_estimate=pl.CostEstimate(flops=2 * 10**9, bytes_accessed=2 * 2**20, transcendentals=0),
        name="chol_inverse",
    )(gram)


def swap(x, axis):
    return lax.all_to_all(x, axis, 0, 0, tiled=True)


def spread(x, axis):
    size = lax.axis_size(axis)
    return swap(jnp.broadcast_to(x[None], (size,) + x.shape), axis)


def two_parts(x):
    high = lax.reduce_precision(x, 8, 7)
    return high.astype(bf16), (x - high).astype(bf16)


def from_parts(x):
    return x[:, :16].astype(f32) + x[:, 16:].astype(f32)


def natural(x):
    return x.reshape(4, 8, 56, RANK).transpose(1, 0, 2, 3).reshape(8 * 4 * 56, RANK)


def on_device(weight, gradient, momentum, basis_in):
    weight_local = weight[0]
    grads = gradient[0].astype(f32)
    basis_low = basis_in[0].astype(bf16)

    basis_z = spread(basis_low, "z").reshape(448, RANK)
    basis_all = natural(lax.all_gather(basis_z, "x", axis=0, tiled=True))
    squares = jnp.full((1, 128), jnp.sum(grads * grads), f32)
    squares, _ = lax.optimization_barrier((squares, basis_z))
    squares = jnp.sum(spread(squares, ("z", "x")), axis=0)
    squares = jnp.sum(spread(squares, "y"), axis=0)
    square_total = lax.psum(squares, "core")[0, 0]

    root_mean = jnp.sqrt(square_total / (2.0 * ROWS * COLS))
    clip_scale = 1.0 / jnp.maximum(1.0, root_mean)
    blend32 = momentum[0].astype(f32) + clip_scale * grads
    blended = blend32.astype(bf16)

    partial_left = jnp.dot(blended, basis_all, preferred_element_type=f32)
    left_rows = jnp.sum(swap(partial_left.reshape(8, 32, RANK), "y"), axis=0)
    left = spread(left_rows, "y").reshape(256, RANK)

    gram_part = lax.dot_general(left, left, TN, precision=HIGHEST)
    gram_part = lax.dynamic_slice_in_dim(
        gram_part.reshape(4, 8, 16, RANK), lax.axis_index("y"), 1, axis=1
    ).reshape(4, 16, RANK)
    high, low = two_parts(left)
    product = lax.dot_general(blended, high, TN, preferred_element_type=f32)
    product = product + lax.dot_general(blended, low, TN, preferred_element_type=f32)
    product = product.astype(bf16).reshape(8, 4, 56, RANK).transpose(1, 0, 2, 3)

    both = jnp.concatenate((product.reshape(4, 448, RANK),) + two_parts(gram_part), axis=1)
    both = swap(both, "x")
    product = jnp.sum(both[:, :448].astype(f32), axis=0).astype(bf16).reshape(8, 56, RANK)
    gram_rows = jnp.concatenate(two_parts(jnp.sum(from_parts(both[:, 448:]), axis=0)), axis=0)
    both = jnp.concatenate((product, jnp.broadcast_to(gram_rows[None], (8, 32, RANK))), axis=1)
    both = swap(both, "z")
    product = jnp.sum(both[:, :56].astype(f32), axis=0)
    gram_rows = jnp.sum(from_parts(both[:, 56:]), axis=0)
    product_all = spread(product.astype(bf16), "x").reshape(224, RANK)
    gram_rows, product_all = lax.optimization_barrier((gram_rows, product_all))
    product_all = lax.all_gather(product_all, "z", axis=0, tiled=True)
    gram_rows = spread(gram_rows, "y").reshape(128, RANK)
    gram_matrix = spread(gram_rows, "x").reshape(RANK, RANK)
    inverse_factor = chol_inverse(gram_matrix)

    high, low = two_parts(inverse_factor)
    right_all = lax.dot_general(product_all, high, NT, preferred_element_type=f32)
    right_all = right_all + lax.dot_general(product_all, low, NT, preferred_element_type=f32)
    column_squares = jnp.sum(right_all * right_all, axis=0, keepdims=True)
    column_squares, inverse_factor = lax.optimization_barrier((column_squares, inverse_factor))

    ortho = lax.dot_general(left, inverse_factor, NT, precision=HIGHEST)
    right_own = lax.dot_general(product, inverse_factor, NT, precision=HIGHEST)
    ortho, right_own = lax.optimization_barrier((ortho, right_own))
    column_squares = jnp.sum(spread(column_squares, "y"), axis=0)
    right_low = right_all.astype(bf16)
    feedback = lax.dot_general(ortho.astype(bf16), right_low, NT, preferred_element_type=f32)
    new_momentum = (blend32 - (1.0 - momentum_keep) * feedback).astype(bf16)
    stretch = math.sqrt(COLS) * lax.rsqrt(column_squares + epsilon)
    new_basis = right_own * stretch
    factor = step_size * math.sqrt(ROWS / RANK)
    update = lax.dot_general(
        (ortho * stretch).astype(bf16), right_low, NT, preferred_element_type=f32
    )
    new_weight = (weight_local.astype(f32) - factor * update).astype(bf16)
    return (new_weight[None], new_momentum[None], new_basis[None])


def solution(mesh):
    devices = mesh.devices.reshape(8, 4, 8, 2)
    fine = Mesh(devices, ("z", "x", "y", "core"))
    matrix = P("core", ("z", "x"), "y")
    basis = P("core", ("y", "z", "x"), None)
    return jax.shard_map(
        on_device,
        mesh=fine,
        in_specs=(matrix, matrix, matrix, basis),
        out_specs=(matrix, matrix, basis),
        check_vma=False,
    )
```

```python
import functools
import math

import jax
import jax.numpy as jnp
from jax import lax
from jax.experimental import pallas as pl
from jax.experimental.pallas import tpu as pltpu
from jax.sharding import Mesh
from jax.sharding import PartitionSpec as P

ROWS = 8192
COLS = 14336
RANK = 512
BLOCK = 128
PIVOTS = 8

momentum_keep = 0.95
step_size = 0.25
epsilon = 1e-06

f32 = jnp.float32
bf16 = jnp.bfloat16
HIGHEST = lax.Precision.HIGHEST
NN = (((1,), (0,)), ((), ()))
TN = (((0,), (0,)), ((), ()))
NT = (((1,), (1,)), ((), ()))


def block_inverse(block):
    tiles = BLOCK // 8
    full = (8, BLOCK)
    work = [block[8 * v : 8 * v + 8, :] for v in range(tiles)]
    row = lax.broadcasted_iota(jnp.int32, full, 0)
    lane = lax.broadcasted_iota(jnp.int32, full, 1)
    inverse = [jnp.where(lane == row + 8 * v, 1.0, 0.0).astype(f32) for v in range(tiles)]
    scale = [None] * tiles

    def across(tile, j):
        return jnp.broadcast_to(tile[:, j : j + 1], full)

    def down(tile, s):
        return jnp.broadcast_to(tile[s : s + 1, :], full)

    for j in range(0, BLOCK, PIVOTS):
        at, s = divmod(j, 8)
        first = [across(work[at], j + a) for a in range(PIVOTS)]
        pivot = [[down(first[b], s + a) for b in range(a + 1)] for a in range(PIVOTS)]
        rows = [down(work[at], s + a) for a in range(PIVOTS)]
        rows_inv = [down(inverse[at], s + a) for a in range(PIVOTS)]
        lower = [[None] * PIVOTS for _ in range(PIVOTS)]
        recip = [None] * PIVOTS
        for a in range(PIVOTS):
            recip[a] = 1.0 / pivot[a][a]
            root = lax.rsqrt(pivot[a][a])
            scale[at] = root if s + a == 0 else jnp.where(row >= s + a, root, scale[at])
            for i in range(a + 1, PIVOTS):
                lower[i][a] = pivot[i][a] * recip[a]
                for b in range(a + 1, i + 1):
                    pivot[i][b] = pivot[i][b] - lower[i][a] * pivot[b][a]
                rows[i] = rows[i] - lower[i][a] * rows[a]
                rows_inv[i] = rows_inv[i] - lower[i][a] * rows_inv[a]
        unit = [rows[a] * recip[a] for a in range(PIVOTS)]
        unit_inv = [rows_inv[a] * recip[a] for a in range(PIVOTS)]
        for v in range(at, tiles):
            column = first if v == at else [across(work[v], j + a) for a in range(PIVOTS)]
            column = list(column)
            for a in range(PIVOTS):
                for i in range(a + 1, PIVOTS):
                    column[i] = column[i] - lower[i][a] * column[a]
            for a in range(PIVOTS):
                factor = column[a]
                if v == at:
                    if s + a == 7:
                        continue
                    factor = jnp.where(row > s + a, factor, 0.0)
                if not (v == at and s + PIVOTS == 8):
                    work[v] = work[v] - factor * unit[a]
                inverse[v] = inverse[v] - factor * unit_inv[a]
    return jnp.concatenate([inverse[v] * scale[v] for v in range(tiles)], axis=0)


def exact(a, b, dims):
    return lax.dot_general(a, b, dims, precision=HIGHEST, preferred_element_type=f32)


def chol_inverse_kernel(gram_ref, out_ref, work_ref):
    work_ref[:, :RANK] = gram_ref[...]
    i = lax.broadcasted_iota(jnp.int32, (RANK, RANK), 0)
    j = lax.broadcasted_iota(jnp.int32, (RANK, RANK), 1)
    work_ref[:, RANK:] = jnp.where(i == j, 1.0, 0.0).astype(f32)
    ahead = gram_ref[:BLOCK, :BLOCK]
    for k in range(0, RANK, BLOCK):
        end = k + BLOCK
        far = end + BLOCK
        left = RANK - far
        inverse = block_inverse(ahead)
        if end == RANK:
            out_ref[k:, :] = exact(inverse, work_ref[k:, end:], NN)
            break
        near = exact(inverse, work_ref[k:end, end:far], NN)
        ahead = work_ref[end:far, end:far] - exact(near, near, TN)
        wide = exact(inverse, work_ref[k:end, far : RANK + end], NN)
        work_ref[end:far, far : RANK + end] = work_ref[end:far, far : RANK + end] - exact(
            near, wide, TN
        )
        if left:
            work_ref[far:, far : RANK + end] = work_ref[far:, far : RANK + end] - exact(
                wide[:, :left], wide, TN
            )
        out_ref[k:end, :end] = wide[:, left:]
        out_ref[k:end, end:] = jnp.zeros((BLOCK, RANK - end), f32)


def chol_inverse(gram):
    return pl.pallas_call(
        chol_inverse_kernel,
        out_shape=jax.ShapeDtypeStruct((RANK, RANK), f32),
        in_specs=[pl.BlockSpec(memory_space=pltpu.VMEM)],
        out_specs=pl.BlockSpec(memory_space=pltpu.VMEM),
        scratch_shapes=[pltpu.VMEM((RANK, 2 * RANK), f32)],
        compiler_params=pltpu.CompilerParams(vmem_limit_bytes=16 * 2**20),
        cost_estimate=pl.CostEstimate(flops=2 * 10**9, bytes_accessed=2 * 2**20, transcendentals=0),
        name="chol_inverse",
    )(gram)


def swap(x, axis):
    return lax.all_to_all(x, axis, 0, 0, tiled=True)


def spread(x, axis):
    size = lax.axis_size(axis)
    return swap(jnp.broadcast_to(x[None], (size,) + x.shape), axis)


def two_parts(x):
    high = lax.reduce_precision(x, 8, 7)
    return high.astype(bf16), (x - high).astype(bf16)


def from_parts(x):
    return x[:, :16].astype(f32) + x[:, 16:].astype(f32)


def natural(x):
    return x.reshape(4, 8, 56, RANK).transpose(1, 0, 2, 3).reshape(8 * 4 * 56, RANK)


def on_device(weight, gradient, momentum, basis_in):
    weight_local = weight[0]
    grads = gradient[0].astype(f32)
    basis_low = basis_in[0].astype(bf16)

    basis_z = spread(basis_low, "z").reshape(448, RANK)
    squares = jnp.full((1, 128), jnp.sum(grads * grads), f32)
    squares = lax.psum(lax.psum(squares, "core"), "x")
    basis_z, squares = lax.optimization_barrier((basis_z, squares))
    basis_x = spread(basis_z, "x")
    squares = lax.psum(lax.psum(squares, "y"), "z")
    basis_x, squares = lax.optimization_barrier((basis_x, squares))
    basis_all = natural(basis_x)
    square_total = squares[0, 0]

    root_mean = jnp.sqrt(square_total / (2.0 * ROWS * COLS))
    clip_scale = 1.0 / jnp.maximum(1.0, root_mean)
    blend32 = momentum[0].astype(f32) + clip_scale * grads
    blended = blend32.astype(bf16)

    partial_left = jnp.dot(blended, basis_all, preferred_element_type=f32)
    left_rows = jnp.sum(swap(partial_left.reshape(8, 32, RANK), "y"), axis=0)
    left = spread(left_rows, "y").reshape(256, RANK)

    gram_part = lax.dot_general(left, left, TN, precision=HIGHEST)
    gram_part = lax.dynamic_slice_in_dim(
        gram_part.reshape(4, 8, 16, RANK), lax.axis_index("y"), 1, axis=1
    ).reshape(4, 16, RANK)
    high, low = two_parts(left)
    product = lax.dot_general(blended, high, TN, preferred_element_type=f32)
    product = product + lax.dot_general(blended, low, TN, preferred_element_type=f32)
    product = product.astype(bf16).reshape(8, 4, 56, RANK).transpose(1, 0, 2, 3)

    both = jnp.concatenate((product.reshape(4, 448, RANK),) + two_parts(gram_part), axis=1)
    both = swap(both, "x")
    product = jnp.sum(both[:, :448].astype(f32), axis=0).astype(bf16).reshape(8, 56, RANK)
    gram_rows = jnp.concatenate(two_parts(jnp.sum(from_parts(both[:, 448:]), axis=0)), axis=0)
    both = jnp.concatenate((product, jnp.broadcast_to(gram_rows[None], (8, 32, RANK))), axis=1)
    both = swap(both, "z")
    product = jnp.sum(both[:, :56].astype(f32), axis=0)
    gram_rows = jnp.sum(from_parts(both[:, 56:]), axis=0)
    product_all = spread(product.astype(bf16), "x").reshape(224, RANK)
    gram_rows, product_all = lax.optimization_barrier((gram_rows, product_all))
    product_all = lax.all_gather(product_all, "z", axis=0, tiled=True)
    gram_rows = spread(gram_rows, "y").reshape(128, RANK)
    gram_matrix = spread(gram_rows, "x").reshape(RANK, RANK)
    inverse_factor = chol_inverse(gram_matrix)

    high, low = two_parts(inverse_factor)
    right_all = lax.dot_general(product_all, high, NT, preferred_element_type=f32)
    right_all = right_all + lax.dot_general(product_all, low, NT, preferred_element_type=f32)
    column_squares = jnp.sum(right_all * right_all, axis=0, keepdims=True)
    column_squares, inverse_factor = lax.optimization_barrier((column_squares, inverse_factor))

    ortho = lax.dot_general(left, inverse_factor, NT, precision=HIGHEST)
    right_own = lax.dot_general(product, inverse_factor, NT, precision=HIGHEST)
    ortho, right_own = lax.optimization_barrier((ortho, right_own))
    column_squares = jnp.sum(spread(column_squares, "y"), axis=0)
    right_low = right_all.astype(bf16)
    feedback = lax.dot_general(ortho.astype(bf16), right_low, NT, preferred_element_type=f32)
    new_momentum = (blend32 - (1.0 - momentum_keep) * feedback).astype(bf16)
    stretch = math.sqrt(COLS) * lax.rsqrt(column_squares + epsilon)
    new_basis = right_own * stretch
    factor = step_size * math.sqrt(ROWS / RANK)
    update = lax.dot_general(
        (ortho * stretch).astype(bf16), right_low, NT, preferred_element_type=f32
    )
    new_weight = (weight_local.astype(f32) - factor * update).astype(bf16)
    return (new_weight[None], new_momentum[None], new_basis[None])


def solution(mesh):
    devices = mesh.devices.reshape(8, 4, 8, 2)
    fine = Mesh(devices, ("z", "x", "y", "core"))
    matrix = P("core", ("z", "x"), "y")
    basis = P("core", ("y", "z", "x"), None)
    return jax.shard_map(
        on_device,
        mesh=fine,
        in_specs=(matrix, matrix, matrix, basis),
        out_specs=(matrix, matrix, basis),
        check_vma=False,
    )
```

```python
import functools
import math

import jax
import jax.numpy as jnp
from jax import lax
from jax.experimental import pallas as pl
from jax.experimental.pallas import tpu as pltpu
from jax.sharding import Mesh
from jax.sharding import PartitionSpec as P

ROWS = 8192
COLS = 14336
RANK = 512
BLOCK = 128
PIVOTS = 8

momentum_keep = 0.95
step_size = 0.25
epsilon = 1e-06

f32 = jnp.float32
bf16 = jnp.bfloat16
HIGHEST = lax.Precision.HIGHEST
NN = (((1,), (0,)), ((), ()))
TN = (((0,), (0,)), ((), ()))
NT = (((1,), (1,)), ((), ()))


def block_inverse(block):
    tiles = BLOCK // 8
    full = (8, BLOCK)
    work = [block[8 * v : 8 * v + 8, :] for v in range(tiles)]
    row = lax.broadcasted_iota(jnp.int32, full, 0)
    lane = lax.broadcasted_iota(jnp.int32, full, 1)
    inverse = [jnp.where(lane == row + 8 * v, 1.0, 0.0).astype(f32) for v in range(tiles)]
    scale = [None] * tiles

    def across(tile, j):
        return jnp.broadcast_to(tile[:, j : j + 1], full)

    def down(tile, s):
        return jnp.broadcast_to(tile[s : s + 1, :], full)

    for j in range(0, BLOCK, PIVOTS):
        at, s = divmod(j, 8)
        first = [across(work[at], j + a) for a in range(PIVOTS)]
        pivot = [[down(first[b], s + a) for b in range(a + 1)] for a in range(PIVOTS)]
        rows = [down(work[at], s + a) for a in range(PIVOTS)]
        rows_inv = [down(inverse[at], s + a) for a in range(PIVOTS)]
        lower = [[None] * PIVOTS for _ in range(PIVOTS)]
        recip = [None] * PIVOTS
        for a in range(PIVOTS):
            recip[a] = 1.0 / pivot[a][a]
            root = lax.rsqrt(pivot[a][a])
            scale[at] = root if s + a == 0 else jnp.where(row >= s + a, root, scale[at])
            for i in range(a + 1, PIVOTS):
                lower[i][a] = pivot[i][a] * recip[a]
                for b in range(a + 1, i + 1):
                    pivot[i][b] = pivot[i][b] - lower[i][a] * pivot[b][a]
                rows[i] = rows[i] - lower[i][a] * rows[a]
                rows_inv[i] = rows_inv[i] - lower[i][a] * rows_inv[a]
        unit = [rows[a] * recip[a] for a in range(PIVOTS)]
        unit_inv = [rows_inv[a] * recip[a] for a in range(PIVOTS)]
        for v in range(at, tiles):
            column = first if v == at else [across(work[v], j + a) for a in range(PIVOTS)]
            column = list(column)
            for a in range(PIVOTS):
                for i in range(a + 1, PIVOTS):
                    column[i] = column[i] - lower[i][a] * column[a]
            for a in range(PIVOTS):
                factor = column[a]
                if v == at:
                    if s + a == 7:
                        continue
                    factor = jnp.where(row > s + a, factor, 0.0)
                if not (v == at and s + PIVOTS == 8):
                    work[v] = work[v] - factor * unit[a]
                inverse[v] = inverse[v] - factor * unit_inv[a]
    return jnp.concatenate([inverse[v] * scale[v] for v in range(tiles)], axis=0)


def exact(a, b, dims):
    return lax.dot_general(a, b, dims, precision=HIGHEST, preferred_element_type=f32)


def chol_inverse_kernel(gram_ref, out_ref, work_ref):
    work_ref[:, :RANK] = gram_ref[...]
    i = lax.broadcasted_iota(jnp.int32, (RANK, RANK), 0)
    j = lax.broadcasted_iota(jnp.int32, (RANK, RANK), 1)
    work_ref[:, RANK:] = jnp.where(i == j, 1.0, 0.0).astype(f32)
    ahead = gram_ref[:BLOCK, :BLOCK]
    for k in range(0, RANK, BLOCK):
        end = k + BLOCK
        far = end + BLOCK
        left = RANK - far
        inverse = block_inverse(ahead)
        if end == RANK:
            out_ref[k:, :] = exact(inverse, work_ref[k:, end:], NN)
            break
        near = exact(inverse, work_ref[k:end, end:far], NN)
        ahead = work_ref[end:far, end:far] - exact(near, near, TN)
        wide = exact(inverse, work_ref[k:end, far : RANK + end], NN)
        work_ref[end:far, far : RANK + end] = work_ref[end:far, far : RANK + end] - exact(
            near, wide, TN
        )
        if left:
            work_ref[far:, far : RANK + end] = work_ref[far:, far : RANK + end] - exact(
                wide[:, :left], wide, TN
            )
        out_ref[k:end, :end] = wide[:, left:]
        out_ref[k:end, end:] = jnp.zeros((BLOCK, RANK - end), f32)


def chol_inverse(gram):
    return pl.pallas_call(
        chol_inverse_kernel,
        out_shape=jax.ShapeDtypeStruct((RANK, RANK), f32),
        in_specs=[pl.BlockSpec(memory_space=pltpu.VMEM)],
        out_specs=pl.BlockSpec(memory_space=pltpu.VMEM),
        scratch_shapes=[pltpu.VMEM((RANK, 2 * RANK), f32)],
        compiler_params=pltpu.CompilerParams(vmem_limit_bytes=16 * 2**20),
        cost_estimate=pl.CostEstimate(flops=2 * 10**9, bytes_accessed=2 * 2**20, transcendentals=0),
        name="chol_inverse",
    )(gram)


def swap(x, axis):
    return lax.all_to_all(x, axis, 0, 0, tiled=True)


def spread(x, axis):
    size = lax.axis_size(axis)
    return swap(jnp.broadcast_to(x[None], (size,) + x.shape), axis)


def two_parts(x):
    high = lax.reduce_precision(x, 8, 7)
    return high.astype(bf16), (x - high).astype(bf16)


def from_parts(x):
    return x[:, :16].astype(f32) + x[:, 16:].astype(f32)


def natural(x):
    return x.reshape(4, 8, 56, RANK).transpose(1, 0, 2, 3).reshape(8 * 4 * 56, RANK)


def on_device(weight, gradient, momentum, basis_in):
    weight_local = weight[0]
    grads = gradient[0].astype(f32)
    basis_low = basis_in[0].astype(bf16)

    basis_z = spread(basis_low, "z").reshape(448, RANK)
    squares = jnp.full((1, 128), jnp.sum(grads * grads), f32)
    squares = lax.psum(lax.psum(lax.psum(squares, "core"), "x"), "y")
    basis_z, squares = lax.optimization_barrier((basis_z, squares))
    basis_x = spread(basis_z, "x")
    squares = lax.psum(squares, "z")
    basis_x, squares = lax.optimization_barrier((basis_x, squares))
    basis_all = natural(basis_x)
    square_total = squares[0, 0]

    root_mean = jnp.sqrt(square_total / (2.0 * ROWS * COLS))
    clip_scale = 1.0 / jnp.maximum(1.0, root_mean)
    blend32 = momentum[0].astype(f32) + clip_scale * grads
    blended = blend32.astype(bf16)

    partial_left = jnp.dot(blended, basis_all, preferred_element_type=f32)
    left_rows = jnp.sum(swap(partial_left.reshape(8, 32, RANK), "y"), axis=0)
    left = spread(left_rows, "y").reshape(256, RANK)

    gram_part = lax.dot_general(left, left, TN, precision=HIGHEST)
    gram_part = lax.dynamic_slice_in_dim(
        gram_part.reshape(4, 8, 16, RANK), lax.axis_index("y"), 1, axis=1
    ).reshape(4, 16, RANK)
    high, low = two_parts(left)
    product = lax.dot_general(blended, high, TN, preferred_element_type=f32)
    product = product + lax.dot_general(blended, low, TN, preferred_element_type=f32)
    product = product.astype(bf16).reshape(8, 4, 56, RANK).transpose(1, 0, 2, 3)

    both = jnp.concatenate((product.reshape(4, 448, RANK),) + two_parts(gram_part), axis=1)
    both = swap(both, "x")
    product = jnp.sum(both[:, :448].astype(f32), axis=0).astype(bf16).reshape(8, 56, RANK)
    gram_rows = jnp.concatenate(two_parts(jnp.sum(from_parts(both[:, 448:]), axis=0)), axis=0)
    both = jnp.concatenate((product, jnp.broadcast_to(gram_rows[None], (8, 32, RANK))), axis=1)
    both = swap(both, "z")
    product = jnp.sum(both[:, :56].astype(f32), axis=0)
    gram_rows = jnp.sum(from_parts(both[:, 56:]), axis=0)
    product_all = spread(product.astype(bf16), "x").reshape(224, RANK)
    gram_rows, product_all = lax.optimization_barrier((gram_rows, product_all))
    product_all = lax.all_gather(product_all, "z", axis=0, tiled=True)
    gram_rows = spread(gram_rows, "y").reshape(128, RANK)
    gram_matrix = spread(gram_rows, "x").reshape(RANK, RANK)
    inverse_factor = chol_inverse(gram_matrix)

    high, low = two_parts(inverse_factor)
    right_all = lax.dot_general(product_all, high, NT, preferred_element_type=f32)
    right_all = right_all + lax.dot_general(product_all, low, NT, preferred_element_type=f32)
    column_squares = jnp.sum(right_all * right_all, axis=0, keepdims=True)
    column_squares, inverse_factor = lax.optimization_barrier((column_squares, inverse_factor))

    ortho = lax.dot_general(left, inverse_factor, NT, precision=HIGHEST)
    right_own = lax.dot_general(product, inverse_factor, NT, precision=HIGHEST)
    ortho, right_own = lax.optimization_barrier((ortho, right_own))
    column_squares = jnp.sum(spread(column_squares, "y"), axis=0)
    right_low = right_all.astype(bf16)
    feedback = lax.dot_general(ortho.astype(bf16), right_low, NT, preferred_element_type=f32)
    new_momentum = (blend32 - (1.0 - momentum_keep) * feedback).astype(bf16)
    stretch = math.sqrt(COLS) * lax.rsqrt(column_squares + epsilon)
    new_basis = right_own * stretch
    factor = step_size * math.sqrt(ROWS / RANK)
    update = lax.dot_general(
        (ortho * stretch).astype(bf16), right_low, NT, preferred_element_type=f32
    )
    new_weight = (weight_local.astype(f32) - factor * update).astype(bf16)
    return (new_weight[None], new_momentum[None], new_basis[None])


def solution(mesh):
    devices = mesh.devices.reshape(8, 4, 8, 2)
    fine = Mesh(devices, ("z", "x", "y", "core"))
    matrix = P("core", ("z", "x"), "y")
    basis = P("core", ("y", "z", "x"), None)
    return jax.shard_map(
        on_device,
        mesh=fine,
        in_specs=(matrix, matrix, matrix, basis),
        out_specs=(matrix, matrix, basis),
        check_vma=False,
    )
```
